32 devices in a mesh: dp: 8 (over y, x, core), mp: 4 (over z).
Axes of the slice: x: 2, y: 2, z: 4, core: 2. Of those that a mesh axis runs over, the one named last changes fastest.
Arguments:
- pyramid: bfloat16 [32, 5440, 256], P(('dp', 'mp')), may hold values from -6 to 6
- proposals: int32 [32, 4, 128], P(('dp', 'mp')), may hold values from 0 to 256, as said below
- levels: int32 [32, 128], P(('dp', 'mp')), may hold values from 0 to 3
- labels: int32 [32, 128], P(('dp', 'mp')), may hold values from 0 to 80, as said below
- targets: int32 [32, 4, 128], P(('dp', 'mp')), may hold values from -64 to 320, as said below
- buckets: int32 [32], P(('dp', 'mp')), may hold values from 0 to 4, as said below
- first_weight: bfloat16 [2, 12544, 1024], P(None, None, 'mp'), may hold values from -0.0546875 to 0.0546875
- first_bias: float32 [2, 1024], replicated, may hold values from -3 to 3
- second_weight: bfloat16 [2, 1024, 1024], replicated, may hold values from -0.1875 to 0.1875
- second_bias: float32 [2, 1024], replicated, may hold values from -3 to 3
- class_weight: bfloat16 [2, 1024, 81], replicated, may hold values from -0.5 to 0.5
- class_bias: float32 [2, 81], replicated, may hold values from -3 to 3
- box_weight: bfloat16 [2, 1024, 4], replicated, may hold values from -0.75 to 0.75
- box_bias: float32 [2, 4], replicated, may hold values from -2 to 2
Outputs:
- scores: float32 [32, 128, 81], P(('dp', 'mp'))
- decoded: float32 [32, 4, 128], P(('dp', 'mp'))
- pyramid_grad: float32 [32, 5440, 256], P(('dp', 'mp'))
- first_weight_grad: float32 [2, 12544, 1024], P(None, None, 'mp')
- first_bias_grad: float32 [2, 1024], replicated
- second_weight_grad: float32 [2, 1024, 1024], replicated
- second_bias_grad: float32 [2, 1024], replicated
- class_weight_grad: float32 [2, 1024, 81], replicated
- class_bias_grad: float32 [2, 81], replicated
- box_weight_grad: float32 [2, 1024, 4], replicated
- box_bias_grad: float32 [2, 4], replicated
The draws below stay inside these ranges and needn't reach their ends.
Inputs may be any that keep to these rules, and one draw needn't show every extreme that they name: `buckets`: some image has bucket 0 and another bucket 4. `proposals`: each box lies in its image, 256 pixels wide and 128 + b * (32) high for bucket b, and is 8 pixels or more wide and high. `targets`: each target is its proposal with every edge moved by at most a quarter of the proposal's extent along that axis. `labels`: 0 is background.
All inputs are finite; a program needn't handle non-finite values.
Results may differ from the reference program's by a relative error of at most 0.033.
Values may be sent and summed in bfloat16 or wider, within the bound.
A program may use at most 384 MiB of HBM per device.

```python
import jax
import jax.numpy as jnp
from jax import lax

CH = 256
HID = 1024
CLS = 81
POOL = 7
SECTIONS = 2
REGIONS = 128
CANVAS = 256
FEAT = 12544
CELLS = 5440
IMAGES = 32
N_MP = 4


def bucket_values(key):
    key = jax.random.fold_in(key, 101)
    key_values, key_high, key_low = jax.random.split(key, 3)
    values = jax.random.randint(key_values, (IMAGES,), 0, 5)
    high_at = jax.random.randint(key_high, (), 0, IMAGES)
    low_at = (high_at + 1 + jax.random.randint(key_low, (), 0, IMAGES - 1)) % IMAGES
    return values.at[high_at].set(4).at[low_at].set(0).astype(jnp.int32)


def proposal_boxes(key):
    bucket_ids = bucket_values(key)
    key = jax.random.fold_in(key, 202)
    keys_all = jax.random.split(key, 4)
    image_height = (CANVAS // 2 + bucket_ids * (CANVAS // 8))[:, None]
    grid_shape = (IMAGES, REGIONS)
    left_edge = jax.random.randint(keys_all[0], grid_shape, 0, CANVAS - 7)
    box_width = jax.random.randint(keys_all[1], grid_shape, 8, CANVAS - left_edge + 1)
    top_edge = jax.random.randint(keys_all[2], grid_shape, 0, image_height - 7)
    box_height = jax.random.randint(keys_all[3], grid_shape, 8, image_height - top_edge + 1)
    return jnp.stack([left_edge, top_edge, left_edge + box_width, top_edge + box_height], axis=1).astype(jnp.int32)


def draw_buckets(key, part):
    return bucket_values(key)


def draw_proposals(key, part):
    return proposal_boxes(key)


def draw_targets(key, part):
    boxes_all = proposal_boxes(key)
    key = jax.random.fold_in(key, 303)
    extent = boxes_all[:, 2:, :] - boxes_all[:, :2, :]
    reach = jnp.concatenate([extent, extent], axis=1) // 4
    moved = jax.random.randint(key, boxes_all.shape, -reach, reach + 1)
    return (boxes_all + moved).astype(jnp.int32)


def draw_labels(key, part):
    key = jax.random.fold_in(key, 404)
    key_fore, key_class = jax.random.split(key)
    foreground = jax.random.randint(key_fore, (IMAGES, REGIONS), 0, 3) == 0
    classes = jax.random.randint(key_class, (IMAGES, REGIONS), 1, CLS)
    return jnp.where(foreground, classes, 0).astype(jnp.int32)


def with_ends(result, rng, least, top_value):
    longest = result.shape.index(max(result.shape))
    spots = []
    for shift in (0, 1):
        where = [jax.random.randint(jax.random.fold_in(rng, axis), (), 0, length) for axis, length in enumerate(result.shape)]
        where[longest] = (where[longest] + shift) % result.shape[longest]
        spots.append(tuple(where))
    return result.at[spots[0]].set(least).at[spots[1]].set(top_value)


def level_of(stream_key, dims, cuts, smallest, high):
    factor_of, own = 1.0, jax.random.fold_in(stream_key, 6)
    for axis_at, shards_of in cuts:
        heights = jnp.exp(jax.random.uniform(jax.random.fold_in(own, axis_at), (shards_of,), jnp.float32, smallest / len(cuts), high / len(cuts)))
        factor_of = factor_of * jnp.repeat(heights, dims[axis_at] // shards_of).reshape([-1 if axis == axis_at else 1 for axis in range(len(dims))])
    return factor_of


def noise(rng, dims, deviation, most, cuts=(), held_as=jnp.bfloat16):
    result = jax.random.normal(rng, dims, jnp.float32) * deviation
    if len(cuts) > 0:
        result = level_of(rng, dims, cuts, -0.22, 0.18) * result
    return jnp.clip(result, min=-most, max=most).astype(held_as)


def setup_inputs(seed: int = 0) -> dict:
    seeds = jax.random.split(jax.random.key(seed), 15)
    return {
        "pyramid": noise(seeds[0], (IMAGES, CELLS, CH), 1.0, 6.0, ((0, 32),)),
        "proposals": draw_proposals(jax.random.fold_in(seeds[14], 71), 0),
        "levels": with_ends(jax.random.randint(seeds[2], (IMAGES, REGIONS), 0, 4), jax.random.fold_in(seeds[2], 1), 0, 3).astype(jnp.int32),
        "labels": draw_labels(jax.random.fold_in(seeds[14], 71), 0),
        "targets": draw_targets(jax.random.fold_in(seeds[14], 71), 0),
        "buckets": draw_buckets(jax.random.fold_in(seeds[14], 71), 0),
        "first_weight": noise(seeds[6], (SECTIONS, FEAT, HID), FEAT ** -0.5, 0.0546875, ((2, 4),)),
        "first_bias": noise(seeds[7], (SECTIONS, HID), 0.5, 3.0, (), jnp.float32),
        "second_weight": noise(seeds[8], (SECTIONS, HID, HID), HID ** -0.5, 0.1875),
        "second_bias": noise(seeds[9], (SECTIONS, HID), 0.5, 3.0, (), jnp.float32),
        "class_weight": noise(seeds[10], (SECTIONS, HID, CLS), (HID // 8) ** -0.5, 0.5),
        "class_bias": noise(seeds[11], (SECTIONS, CLS), 0.5, 3.0, (), jnp.float32),
        "box_weight": noise(seeds[12], (SECTIONS, HID, 4), (HID // 16) ** -0.5, 0.75),
        "box_bias": noise(seeds[13], (SECTIONS, 4), 0.3, 2.0, (), jnp.float32),
    }


@jax.custom_vjp
def low(v):
    return lax.optimization_barrier(v.astype(jnp.bfloat16)).astype(jnp.float32)

@jax.custom_vjp
def low_back(v):
    return v

def low_keep(v):
    return (low(v), None)

def low_pass(kept, grad):
    return (grad,)

def back_keep(v):
    return (v, None)

def back_low(kept, grad):
    return (low(grad),)
low.defvjp(low_keep, low_pass)
low_back.defvjp(back_keep, back_low)

def product(left_side, right_side):
    return jnp.dot(left_side, right_side, precision=lax.Precision.HIGHEST, preferred_element_type=jnp.float32)

def sample_table(corners, level_ids):
    stride_list = [4 << level_no for level_no in range(4)]
    side_list = [CANVAS // stride_value for stride_value in stride_list]
    offset_list = [sum((side_value * side_value for side_value in side_list[:level_no])) for level_no in range(4)]
    onehot = level_ids[:, None] == jnp.arange(4, dtype=jnp.int32)[None, :]
    inverse = lax.optimization_barrier(jnp.sum(jnp.where(onehot, jnp.array([1.0 / stride_value for stride_value in stride_list], jnp.float32)[None, :], 0.0), axis=1))
    side_cells = lax.optimization_barrier(jnp.sum(jnp.where(onehot, jnp.array(side_list, jnp.int32)[None, :], 0), axis=1)).astype(jnp.int32)
    level_offset = lax.optimization_barrier(jnp.sum(jnp.where(onehot, jnp.array(offset_list, jnp.int32)[None, :], 0), axis=1)).astype(jnp.int32)
    fractions = (jnp.arange(POOL, dtype=jnp.float32) + 0.5) / POOL

    def axis_points(begin, finish):
        points = (begin[:, None] + fractions[None, :] * (finish - begin)[:, None]) * inverse[:, None] - 0.5
        points = jnp.clip(points, 0.0, (side_cells - 1).astype(points.dtype)[:, None])
        lower_cell = jnp.minimum(jnp.floor(points).astype(jnp.int32), side_cells[:, None] - 2)
        return (lower_cell, points - lower_cell.astype(points.dtype))
    col_low, col_frac = axis_points(corners[0], corners[2])
    row_low, row_frac = axis_points(corners[1], corners[3])
    side_three = side_cells[:, None, None]
    base_cell = level_offset[:, None, None] + row_low[:, :, None] * side_three + col_low[:, None, :]
    cell_index = jnp.stack([base_cell, base_cell + 1, base_cell + side_three, base_cell + side_three + 1], axis=-1)
    row_weight = row_frac[:, :, None]
    col_weight = col_frac[:, None, :]
    weights = jnp.stack([(1.0 - row_weight) * (1.0 - col_weight), (1.0 - row_weight) * col_weight, row_weight * (1.0 - col_weight), row_weight * col_weight], axis=-1)
    regions = corners.shape[1]
    return (cell_index.reshape(regions, POOL * POOL, 4).astype(jnp.int32), weights.reshape(regions, POOL * POOL, 4))

def box_frame(corners):
    box_width = corners[2] - corners[0]
    box_height = corners[3] - corners[1]
    return (corners[0] + 0.5 * box_width, corners[1] + 0.5 * box_height, box_width, box_height)

def encode_boxes(corners, truth_boxes, factor):
    centre_col, centre_row, box_width, box_height = box_frame(corners)
    truth_col, truth_row, truth_width, truth_height = box_frame(truth_boxes)
    return jnp.stack([10.0 * factor * (truth_col - centre_col) / box_width, 10.0 * factor * (truth_row - centre_row) / box_height, 5.0 * factor * jnp.log(truth_width / box_width), 5.0 * factor * jnp.log(truth_height / box_height)], axis=1)

def decode_boxes(corners, deltas, factor):
    centre_col, centre_row, box_width, box_height = box_frame(corners)
    moved_col = centre_col + deltas[:, 0] / (10.0 * factor) * box_width
    moved_row = centre_row + deltas[:, 1] / (10.0 * factor) * box_height
    moved_width = box_width * jnp.exp(deltas[:, 2] / (5.0 * factor))
    moved_height = box_height * jnp.exp(deltas[:, 3] / (5.0 * factor))
    return jnp.stack([moved_col - 0.5 * moved_width, moved_row - 0.5 * moved_height, moved_col + 0.5 * moved_width, moved_row + 0.5 * moved_height], axis=0)

def section_head(params, section_no, feature, corners, level_ids):
    first_w, first_b, second_w, second_b, class_w, class_b, box_w, box_b = params
    cell_index, weights = sample_table(corners, level_ids)
    gathered = feature[cell_index]
    pooled = jnp.einsum('rbk,rbkc->rbc', weights, gathered, precision=lax.Precision.HIGHEST)
    pooled = low(pooled.reshape(corners.shape[1], POOL * POOL * CH))
    part_width = HID // N_MP
    pieces = [product(low_back(pooled), first_w[section_no][:, shard_no * part_width:(shard_no + 1) * part_width]) for shard_no in range(N_MP)]
    first_pre = low_back(jnp.concatenate(pieces, axis=1) + first_b[section_no])
    first_act = low_back(low(jax.nn.gelu(first_pre)))
    second_pre = low_back(product(first_act, second_w[section_no]) + second_b[section_no])
    second_act = low(jax.nn.gelu(second_pre))
    logits = low_back(product(second_act, class_w[section_no]) + class_b[section_no])
    deltas = low_back(product(second_act, box_w[section_no]) + box_b[section_no])
    return (logits, deltas)

def section_loss(logits, deltas, goal_deltas, label_ids, live_rows, live_count):
    log_probs = jax.nn.log_softmax(logits, axis=1)
    onehot = label_ids[:, None] == jnp.arange(CLS, dtype=jnp.int32)[None, :]
    cross = -lax.optimization_barrier(jnp.sum(jnp.where(onehot, log_probs, 0.0), axis=1))
    differ = deltas - goal_deltas
    magnitude = jnp.abs(differ)
    huber = lax.optimization_barrier(jnp.sum(jnp.where(magnitude < 1.0, 0.5 * differ * differ, magnitude - 0.5), axis=1))
    moving = jnp.logical_and(live_rows, label_ids > 0)
    return (jnp.sum(jnp.where(live_rows, cross, 0.0)) + jnp.sum(jnp.where(moving, huber, 0.0))) / live_count

def reference(pyramid, proposals, levels, labels, targets, buckets, first_weight, first_bias, second_weight, second_bias, class_weight, class_bias, box_weight, box_bias):
    params = (first_weight.astype(jnp.float32), first_bias.astype(jnp.float32), second_weight.astype(jnp.float32), second_bias.astype(jnp.float32), class_weight.astype(jnp.float32), class_bias.astype(jnp.float32), box_weight.astype(jnp.float32), box_bias.astype(jnp.float32))
    features = pyramid.astype(jnp.float32)
    first_boxes = proposals.astype(jnp.float32)
    truth_all = targets.astype(jnp.float32)

    def first_pass(record):
        feature, corners, level_ids = record
        logits, deltas = section_head(params, 0, feature, corners, level_ids)
        return decode_boxes(corners, deltas, 1.0)
    second_boxes = lax.map(first_pass, (features, first_boxes, levels))

    def image_loss(weights_all, record):
        feature, corners_one, corners_two, level_ids, label_ids, truth_boxes, bucket_id = record
        live_rows = jnp.arange(REGIONS, dtype=jnp.int32) < REGIONS // 2 + bucket_id * (REGIONS // 8)
        live_count = jnp.sum(live_rows.astype(jnp.float32))
        logits_one, deltas_one = section_head(weights_all, 0, feature, corners_one, level_ids)
        loss_one = section_loss(logits_one, deltas_one, encode_boxes(corners_one, truth_boxes, 1.0), label_ids, live_rows, live_count)
        logits_two, deltas_two = section_head(weights_all, 1, feature, corners_two, level_ids)
        loss_two = section_loss(logits_two, deltas_two, encode_boxes(corners_two, truth_boxes, 2.0), label_ids, live_rows, live_count)
        return (loss_one + loss_two, (jax.nn.softmax(logits_two, axis=1), decode_boxes(corners_two, deltas_two, 2.0)))

    def whole(weights_all, feature_all):

        def per_image(record):
            return jax.checkpoint(image_loss)(weights_all, record)
        losses, outputs = lax.map(per_image, (feature_all, first_boxes, second_boxes, levels, labels, truth_all, buckets))
        return (jnp.sum(losses), outputs)
    loss, pullback, outputs = jax.vjp(whole, params, features, has_aux=True)
    weight_grads, feature_grad = pullback(jnp.ones_like(loss))
    return (outputs[0], outputs[1], feature_grad / 3.0, weight_grads[0], weight_grads[1], weight_grads[2], weight_grads[3], weight_grads[4], weight_grads[5], weight_grads[6], weight_grads[7])
```

```python
import functools
import math

import jax
import jax.numpy as jnp
from jax import lax
from jax.experimental import pallas as pl
from jax.experimental.pallas import tpu as pltpu
from jax.sharding import Mesh
from jax.sharding import PartitionSpec as P

CH = 256
CLS = 81
POOL = 7
BINS = POOL * POOL
CANVAS = 256
FEAT = BINS * CH
LANE = 128
UNITS = FEAT // LANE
SIDES = [CANVAS // (4 << level_no) for level_no in range(4)]
CELLS = 5440
ROWS_IN = [16, 32, 16, 8]
OFFSET = [0, 4096, 5120, 5376]
COUNT = [4, 1, 1, 1]
GROUP = 16
SMALL = pl.CostEstimate(flops=1000, bytes_accessed=1000, transcendentals=0)


def hat(distance):
    return jnp.maximum(1.0 - jnp.abs(distance), 0.0)


def cell_block(level_no, block_no):
    cells = ROWS_IN[level_no] * SIDES[level_no]
    return pl.ds(pl.multiple_of(OFFSET[level_no] + block_no * cells, min(cells, CH)), cells)


def lane_points(params):
    width = BINS * GROUP
    flat = params[...].T[:8]
    pieces = []
    for unused in range(3):
        pieces.append(flat.astype(jnp.bfloat16))
        flat = flat - pieces[-1].astype(jnp.float32)
    region = lax.broadcasted_iota(jnp.int32, (GROUP, width), 0)
    lane = lax.broadcasted_iota(jnp.int32, (GROUP, width), 1)
    chosen = (region == (lane & (GROUP - 1))).astype(jnp.bfloat16)
    wide = sum(jnp.dot(piece, chosen, preferred_element_type=jnp.float32) for piece in pieces)
    bin_no = lax.broadcasted_iota(jnp.int32, (1, width), 1) // GROUP
    across = bin_no // POOL
    down = bin_no - across * POOL

    def place(begin, extent, number):
        fraction = (number.astype(jnp.float32) + 0.5) * (1.0 / POOL)
        return jnp.clip(begin + fraction * extent, 0.0, wide[4:5])

    return place(wide[0:1], wide[1:2], down), place(wide[2:3], wide[3:4], across), wide[5:6]


def spread_kernel(unit_places, scale, groups, bounds, params, first, second, out, table, stack):
    group_no = pl.program_id(0)
    col_row, row_row, level_row = lane_points(params)

    @pl.when(group_no == 0)
    def _():
        out[...] = jnp.zeros_like(out)

    def fill(grads):
        for unit_no in range(UNITS):
            bin_no, half = divmod(unit_no, 2)
            owner, place = unit_places[unit_no]
            stack[bin_no * GROUP : (bin_no + 1) * GROUP, half * LANE : (half + 1) * LANE] = grads[
                owner, :, place * LANE : (place + 1) * LANE
            ]

    @pl.when(group_no < groups)
    def _():
        fill(first)

    @pl.when(group_no >= groups)
    def _():
        fill(second)

    for level_no in range(4):
        side = SIDES[level_no]
        begin = bounds[group_no, level_no]
        finish = bounds[group_no, 4 + level_no]

        @pl.when(finish > begin)
        def _():
            span = lax.broadcasted_iota(jnp.int32, (side, BINS * GROUP), 0).astype(jnp.float32)
            table[:side] = jnp.where(level_row == level_no, hat(span - col_row) * scale, 0.0)

        many = ROWS_IN[level_no]

        def step(chunk_no, carry):
            first_row = chunk_no * many
            weights = jnp.concatenate(
                [
                    table[:side] * hat((first_row + row_no).astype(jnp.float32) - row_row)
                    for row_no in range(many)
                ],
                axis=0,
            ).astype(jnp.bfloat16)
            at = cell_block(level_no, chunk_no)
            out[at, :] += jnp.dot(weights, stack[...], preferred_element_type=jnp.float32)
            return carry

        lax.fori_loop(begin, finish, step, 0)


def gelu_slope(preact):
    scale = math.sqrt(2.0 / math.pi)
    square = preact * preact
    bent = jnp.tanh(scale * preact * (1.0 + 0.044715 * square))
    return 0.5 * (1.0 + bent) + 0.5 * preact * (1.0 - bent * bent) * scale * (
        1.0 + 3.0 * 0.044715 * square
    )


def region_params(corners, level):
    regions = level.shape[0]
    inverse = jnp.where(
        level < 0.5, 0.25, jnp.where(level < 1.5, 0.125, jnp.where(level < 2.5, 0.0625, 0.03125))
    )
    most = CANVAS * inverse - 1.0
    begin_col = corners[0] * inverse - 0.5
    begin_row = corners[1] * inverse - 0.5
    extent_col = (corners[2] - corners[0]) * inverse
    extent_row = (corners[3] - corners[1]) * inverse
    lane = lax.broadcasted_iota(jnp.int32, (regions, LANE), 1)
    params = jnp.zeros((regions, LANE), jnp.float32)
    for place, column in enumerate((begin_col, extent_col, begin_row, extent_row, most, level)):
        params = jnp.where(lane == place, column, params)

    one = begin_row + extent_row * (0.5 / POOL)
    other = begin_row + extent_row * ((POOL - 0.5) / POOL)
    low = jnp.floor(jnp.clip(jnp.minimum(one, other) - 0.001, 0.0, most))
    high = jnp.minimum(jnp.floor(jnp.clip(jnp.maximum(one, other) + 0.001, 0.0, most)) + 1.0, most)
    lane_level = (lane & 3).astype(jnp.float32)
    per_row = jnp.where(lane_level == 1.0, 1.0 / 32, jnp.where(lane_level == 3.0, 1.0 / 8, 1.0 / 16))
    member = level == lane_level
    low = jnp.where(member, jnp.floor(low * per_row), 64.0)
    high = jnp.where(member, jnp.floor(high * per_row) + 1.0, 0.0)
    groups = regions // GROUP
    low = jnp.min(low.reshape(groups, GROUP, LANE), axis=1)
    high = jnp.max(high.reshape(groups, GROUP, LANE), axis=1)
    lane = lax.broadcasted_iota(jnp.int32, (groups, LANE), 1)
    level_no = lane & 3
    limit = jnp.where(level_no == 0, float(COUNT[0]), 1.0)
    bounds = jnp.where(lane < 4, jnp.clip(low, 0.0, limit), jnp.clip(high, 0.0, limit))
    return params, bounds.astype(jnp.int32)


def columns_of(info, first, number=1):
    return [info[:, at : at + 1] for at in range(first, first + number)]


def head_kernel(
    factor, parts, first_bias, second_weight, second_bias, out_weight, out_bias, info,
    first_pre, second_pre, acts, heads, moved, params, bounds,
):
    hidden = first_bias.shape[1]
    pre = first_bias[...] + parts[0].astype(jnp.float32)
    for owner in range(1, parts.shape[0]):
        pre = pre + parts[owner].astype(jnp.float32)
    first_pre[...] = pre
    act = jax.nn.gelu(pre).astype(jnp.bfloat16)
    share = hidden // acts.shape[0]
    for owner in range(acts.shape[0]):
        acts[owner, :, :share] = act[:, owner * share : (owner + 1) * share]
    pre = jnp.dot(act, second_weight[...], preferred_element_type=jnp.float32) + second_bias[...]
    second_pre[...] = pre
    act = jax.nn.gelu(pre).astype(jnp.bfloat16)
    for owner in range(acts.shape[0]):
        acts[owner, :, share:] = act[:, owner * share : (owner + 1) * share]
    head = jnp.dot(act, out_weight[...], preferred_element_type=jnp.float32) + out_bias[...]
    heads[...] = head
    corners = columns_of(info, 0, 4)
    deltas = [head[:, CLS + at : CLS + at + 1] for at in range(4)]
    centre_col, centre_row, box_width, box_height = box_frame(corners)
    moved_col = centre_col + deltas[0] / (10.0 * factor) * box_width
    moved_row = centre_row + deltas[1] / (10.0 * factor) * box_height
    moved_width = box_width * jnp.exp(deltas[2] / (5.0 * factor))
    moved_height = box_height * jnp.exp(deltas[3] / (5.0 * factor))
    corners = (
        moved_col - 0.5 * moved_width,
        moved_row - 0.5 * moved_height,
        moved_col + 0.5 * moved_width,
        moved_row + 0.5 * moved_height,
    )
    table = info[...]
    lane = lax.broadcasted_iota(jnp.int32, table.shape, 1)
    for place, column in enumerate(corners):
        table = jnp.where(lane == place, column, table)
    moved[...] = table
    values, chunks = region_params(corners, info[:, 8:9])
    params[...] = values
    bounds[...] = chunks


def head_back_kernel(
    factor, first_pre, second_pre, heads, info, second_weight, out_weight, grads, probs
):
    hidden = first_pre.shape[1]
    corners = columns_of(info, 0, 4)
    truth = columns_of(info, 4, 4)
    label, live, live_count, moving = columns_of(info, 9, 4)
    centre_col, centre_row, box_width, box_height = box_frame(corners)
    truth_col, truth_row, truth_width, truth_height = box_frame(truth)
    goals = (
        10.0 * factor * (truth_col - centre_col) / box_width,
        10.0 * factor * (truth_row - centre_row) / box_height,
        5.0 * factor * jnp.log(truth_width / box_width),
        5.0 * factor * jnp.log(truth_height / box_height),
    )
    head = heads[...]
    lane = lax.broadcasted_iota(jnp.int32, head.shape, 1)
    logits = jnp.where(lane < CLS, head, -jnp.inf)
    shifted = jnp.exp(logits - jnp.max(logits, axis=1, keepdims=True))
    share = shifted / jnp.sum(shifted, axis=1, keepdims=True)
    probs[...] = share
    onehot = (lane == label.astype(jnp.int32)).astype(jnp.float32)
    goal = jnp.zeros_like(head)
    for place, column in enumerate(goals):
        goal = jnp.where(lane == CLS + place, column, goal)
    dhead = jnp.where(
        lane < CLS,
        live * (share - onehot) / live_count,
        jnp.where(
            lane < CLS + 4, moving * jnp.clip(head - goal, -1.0, 1.0) / live_count, 0.0
        ),
    ).astype(jnp.bfloat16)
    grads[:, 2 * hidden :] = dhead
    across = (((1,), (1,)), ((), ()))
    dact = lax.dot_general(dhead, out_weight[...], across, preferred_element_type=jnp.float32)
    dpre = (gelu_slope(second_pre[...]) * dact).astype(jnp.bfloat16)
    grads[:, hidden : 2 * hidden] = dpre
    dact = lax.dot_general(dpre, second_weight[...], across, preferred_element_type=jnp.float32)
    dact = dact.astype(jnp.bfloat16).astype(jnp.float32)
    grads[:, :hidden] = (gelu_slope(first_pre[...]) * dact).astype(jnp.bfloat16)


def plane_place(device, shard):
    return {"plane": lax.div(device, 2), "core": lax.rem(device, 2), "mp": shard}


def half_of(ref, which):
    size = ref.shape[0] // 2
    return ref.at[pl.ds(which * size, size)]


def plane_gather(chips, shard, source, target, sems, local_sem):
    core = lax.axis_index("core")
    chip = lax.axis_index("plane")
    me = chip * 2 + core

    def send(kind, block, place, target_chip, target_core):
        return pltpu.make_async_remote_copy(
            src_ref=block, dst_ref=place,
            send_sem=sems.at[0, kind], recv_sem=sems.at[1, kind],
            device_id=plane_place(target_chip * 2 + target_core, shard),
            device_id_type=pl.DeviceIdType.MESH,
        )

    def beside(kind, held):
        slot = held * 2 + core
        block = source if kind == 0 else target.at[slot]
        return send(kind, block, target.at[slot], chip, 1 - core)

    own = pltpu.make_async_copy(source, target.at[me], local_sem)

    if chips == 4:
        near = chip + 1 - 2 * lax.rem(chip, 2)
        other = lax.rem(chip + 2, 4)
        far = 3 - chip
        first = send(4, source, target.at[me], near, core)
        second = send(5, source, target.at[me], other, core)
        place = half_of(target.at[near * 2 + core], 0)
        first_on = send(6, place, place, other, core)
        place = half_of(target.at[other * 2 + core], 1)
        second_on = send(7, place, place, near, core)
        asides = [beside(kind, held) for kind, held in enumerate((chip, near, other, far))]

        def start():
            first.start()
            second.start()
            asides[0].start()
            own.start()

        def relay():
            first.wait_recv()
            first_on.start()
            second.wait_recv()
            second_on.start()
            asides[1].start()
            asides[2].start()

        def last():
            first_on.wait_recv()
            second_on.wait_recv()
            asides[3].start()

        def end():
            own.wait()
            for copy in (first, second, first_on, second_on):
                copy.wait_send()
            for copy in asides:
                copy.wait()

        return start, relay, last, end

    straight = [
        send(chips + step, source, target.at[me], lax.rem(chip + step, chips), core)
        for step in range(1, chips)
    ]
    asides = [beside(step, lax.rem(chip - step + chips, chips)) for step in range(chips)]

    def start():
        for copy in straight:
            copy.start()
        asides[0].start()
        own.start()

    def relay():
        for step in range(1, chips):
            straight[step - 1].wait_recv()
            asides[step].start()

    def last():
        pass

    def end():
        own.wait()
        for copy in straight:
            copy.wait_send()
        for copy in asides:
            copy.wait()

    return start, relay, last, end


def pool_one(group_no, unit_places, params, maps, out, cols, rows, table, total):
    place = pl.ds(pl.multiple_of(group_no * GROUP, GROUP), GROUP)
    begin_col, extent_col, begin_row, extent_row, most, level = [
        jnp.broadcast_to(params[place, at : at + 1], (GROUP, LANE)) for at in range(6)
    ]
    for bin_no in range(POOL):
        fraction = (bin_no + 0.5) / POOL
        cols[bin_no] = jnp.clip(begin_col + fraction * extent_col, 0.0, most)
        rows[bin_no] = jnp.clip(begin_row + fraction * extent_row, 0.0, most)
    lane = lax.broadcasted_iota(jnp.int32, (GROUP, LANE), 1)
    total[...] = jnp.zeros_like(total)
    for level_no in range(4):
        side = SIDES[level_no]
        span = (lane % side).astype(jnp.float32)
        for bin_no in range(POOL):
            table[bin_no] = jnp.where(level == level_no, hat(span - cols[bin_no]), 0.0)
        cells = ROWS_IN[level_no] * side

        def step(block_no, carry):
            first_row = (block_no * ROWS_IN[level_no]).astype(jnp.float32)
            tiles = []
            for tile in range(-(-cells // LANE)):
                at = (lane // side + tile * (LANE // side)).astype(jnp.float32) + first_row
                parts = []
                for i in range(POOL):
                    weight = hat(at - rows[i])
                    parts += [weight * table[j] for j in range(POOL)]
                tiles.append(jnp.concatenate(parts, axis=0).astype(jnp.bfloat16))
            weights = tiles[0] if len(tiles) == 1 else jnp.concatenate(tiles, axis=1)
            total[...] += jnp.dot(
                weights[:, :cells],
                maps[cell_block(level_no, block_no), :],
                preferred_element_type=jnp.float32,
            )
            return carry

        lax.fori_loop(0, COUNT[level_no], step, 0)
    for unit_no in range(UNITS):
        bin_no, half = divmod(unit_no, 2)
        owner, at = unit_places[unit_no]
        out[owner, place, at * LANE : (at + 1) * LANE] = total[
            bin_no * GROUP : (bin_no + 1) * GROUP, half * LANE : (half + 1) * LANE
        ].astype(jnp.bfloat16)


def weight_line(me, shard, first_weight, weight, line_sem, own_sem):
    shards, depth, width = weight.shape
    first_row = pl.multiple_of(jnp.minimum(me * depth, FEAT - depth), LANE)
    slice_here = first_weight.at[pl.ds(first_row, depth)]
    own = pltpu.make_async_copy(slice_here, weight.at[shard], own_sem)

    def send(way, step):
        if way == 0:
            block, target = lax.rem(shard - step + shards, shards), lax.rem(shard + 1, shards)
        else:
            block, target = lax.rem(shard + step, shards), lax.rem(shard + shards - 1, shards)
        return pltpu.make_async_remote_copy(
            src_ref=slice_here if step == 0 else weight.at[block], dst_ref=weight.at[block],
            send_sem=line_sem.at[0, way, step], recv_sem=line_sem.at[1, way, step],
            device_id=plane_place(me, target), device_id_type=pl.DeviceIdType.MESH,
        )

    def start():
        @pl.when(shard < shards - 1)
        def _():
            send(0, 0).start()

        @pl.when(shard > 0)
        def _():
            send(1, 0).start()

        own.start()

    def turn(step):
        @pl.when(shard >= step)
        def _():
            send(0, step - 1).wait_recv()

            @pl.when(shard < shards - 1)
            def _():
                send(0, step).start()

        @pl.when(shard + step < shards)
        def _():
            send(1, step - 1).wait_recv()

            @pl.when(shard > 0)
            def _():
                send(1, step).start()

    def end():
        own.wait()
        for step in range(shards):

            @pl.when(jnp.logical_and(shard >= step, shard < shards - 1))
            def _():
                send(0, step).wait_send()

            @pl.when(jnp.logical_and(shard + step < shards, shard > 0))
            def _():
                send(1, step).wait_send()

    return start, turn, end


def cascade_kernel(
    owners, shards,
    info, maps, first_weight, first_bias, second_weight, second_bias, out_weight, out_bias,
    moved, probs, all_params, all_bounds,
    first_back, second_back, slices, second_final, first_heads, second_heads,
    weights, second_held, pooled, gots, between, spare_probs, spare_params, spare_bounds,
    whole, sent, beside, added, parts, first_pre, second_pre, heads, grads, acts,
    grads_all, acts_all, own_sums, rising, falling, final, extra, mixed,
    cols, rows_at, table, total,
    line_sem, pooled_sem, side_sem, part_sem, grad_sem, acts_sem, back_sem, rise_sem, fall_sem,
    free_sem, slice_sem, mixed_sem, head_sem, local_sem,
):
    mesh_type = pl.DeviceIdType.MESH
    shard = lax.axis_index("mp")
    core = lax.axis_index("core")
    chip = lax.axis_index("plane")
    chips = owners // 2
    me = chip * 2 + core
    regions, hidden = first_pre.shape
    depth = pooled.shape[2]
    half = regions // 2
    rows, width = own_sums.shape[1:]
    each, unit_places = unit_table(owners)

    def peer(step):
        return lax.rem(me + step, owners)

    def chip_before(step):
        return lax.rem(chip - step + chips, chips)

    second_load = [
        pltpu.make_async_copy(second_weight.at[section], second_held, local_sem.at[0])
        for section in range(2)
    ]
    second_load[0].start()
    barrier = pltpu.get_barrier_semaphore()
    for step in range(1, owners):
        pl.semaphore_signal(
            barrier, inc=1, device_id=plane_place(peer(step), shard), device_id_type=mesh_type
        )
    for step in range(1, shards):
        pl.semaphore_signal(
            barrier, inc=1, device_id=plane_place(me, lax.rem(shard + step, shards)),
            device_id_type=mesh_type,
        )
    pl.semaphore_wait(barrier, owners + shards - 2)
    lines = [
        weight_line(
            me, shard, first_weight.at[section], weights.at[section], line_sem.at[section],
            local_sem.at[1 + section],
        )
        for section in range(2)
    ]

    def pooled_copy(section, step, side, batch):
        target = lax.rem(chip + step, chips) * 2 + (core if side == 0 else 1 - core)
        place = pl.ds(batch * half, half)
        at = 2 * step + side
        return pltpu.make_async_remote_copy(
            src_ref=pooled.at[target, place], dst_ref=gots.at[section, me, place],
            send_sem=pooled_sem.at[0, section, batch, at],
            recv_sem=pooled_sem.at[1, section, batch, at],
            device_id=plane_place(target, shard), device_id_type=mesh_type,
        )

    def pooled_own(section, batch):
        place = pl.ds(batch * half, half)
        return pltpu.make_async_copy(
            pooled.at[me, place], gots.at[section, me, place], local_sem.at[3 + batch]
        )

    def pooled_send(section, batch):
        for step in range(chips):
            for side in range(2):
                if step + side:
                    pooled_copy(section, step, side, batch).start()
        pooled_own(section, batch).start()

    def side_copy(section, step):
        source = chip_before(step)
        return pltpu.make_async_remote_copy(
            src_ref=sent.at[source], dst_ref=beside.at[source],
            send_sem=side_sem.at[0, section, step], recv_sem=side_sem.at[1, section, step],
            device_id=plane_place(chip * 2 + 1 - core, shard), device_id_type=mesh_type,
        )

    def part_copy(section, step):
        source = chip_before(step)
        return pltpu.make_async_remote_copy(
            src_ref=added.at[source], dst_ref=parts.at[chip],
            send_sem=part_sem.at[0, section, step], recv_sem=part_sem.at[1, section, step],
            device_id=plane_place(source * 2 + core, shard), device_id_type=mesh_type,
        )

    def acts_copy(section, step):
        target = peer(step)
        return pltpu.make_async_remote_copy(
            src_ref=acts.at[target], dst_ref=acts_all.at[me],
            send_sem=acts_sem.at[0, section, step], recv_sem=acts_sem.at[1, section, step],
            device_id=plane_place(target, shard), device_id_type=mesh_type,
        )

    def acts_own(section):
        return pltpu.make_async_copy(acts.at[me], acts_all.at[me], local_sem.at[5 + section])

    def multiply(section, source):
        place = pl.ds(source * 2, 2)
        block = gots[section, place].reshape(2 * regions, depth)

        def columns(at, carry):
            place = pl.ds(pl.multiple_of(at * width, LANE), width)
            product = jnp.dot(block, weights[section, at], preferred_element_type=jnp.float32)
            for which in range(2):
                part = product[which * regions : (which + 1) * regions]

                @pl.when(core == which)
                def _():
                    whole[source, :, place] = part

                @pl.when(core != which)
                def _():
                    sent[source, :, place] = part.astype(jnp.bfloat16)

            return carry

        lax.fori_loop(0, shards, columns, 0)

    def combine(section, step):
        source = chip_before(step)
        side_copy(section, step).wait_recv()
        added[source] = (whole[source] + beside[source].astype(jnp.float32)).astype(jnp.bfloat16)

        @pl.when(step > 0)
        def _():
            part_copy(section, step).start()

    def first_layer(section):
        for batch in range(2):
            pooled_own(section, batch).wait()

        def arrive(step, carry):
            for batch in range(2):

                @pl.when(step > 0)
                def _():
                    pooled_copy(section, step, 0, batch).wait_recv()

                pooled_copy(section, step, 1, batch).wait_recv()
            multiply(section, chip_before(step))
            side_copy(section, step).start()

            @pl.when(step > 0)
            def _():
                combine(section, step - 1)

            return carry

        lax.fori_loop(0, chips, arrive, 0)
        combine(section, chips - 1)

    def first_sums(section):
        def settle(step, carry):
            side_copy(section, step).wait_send()
            for batch in range(2):
                pooled_copy(section, step, 1, batch).wait_send()

                @pl.when(step > 0)
                def _():
                    pooled_copy(section, step, 0, batch).wait_send()

            @pl.when(step > 0)
            def _():
                part_copy(section, step).wait()

            return carry

        lax.fori_loop(0, chips, settle, 0)
        parts[chip] = added[chip]

    def gather_of(section):
        return plane_gather(
            chips, shard, grads, grads_all, grad_sem.at[section], local_sem.at[7 + section]
        )

    def head(section, table_in, table_out, params_out, bounds_out, probs_out):
        one = pl.ds(section, 1)
        head_kernel(
            section + 1.0, parts, first_bias.at[one], second_held, second_bias.at[one],
            out_weight.at[section], out_bias.at[one], table_in,
            first_pre, second_pre, acts, heads, table_out, params_out, bounds_out,
        )
        for step in range(1, owners):
            acts_copy(section, step).start()
        acts_own(section).start()
        head_back_kernel(
            section + 1.0, first_pre, second_pre, heads, table_in, second_held,
            out_weight.at[section], grads, probs_out,
        )

    def acts_end(section):
        acts_own(section).wait()
        for step in range(1, owners):
            acts_copy(section, step).wait()

    def pool(section, first, last):
        def step(group_no, carry):
            pool_one(
                group_no, unit_places, all_params.at[section], maps, pooled,
                cols, rows_at, table, total,
            )
            return carry

        lax.fori_loop(first, last, step, 0)

    groups = regions // GROUP
    quarter = groups // 4

    lines[0][0]()
    values, chunks = region_params(columns_of(info, 0, 4), info[:, 8:9])
    all_params[0] = values
    all_bounds[0] = chunks
    for owner in range(owners):
        taken = [place for who, place in unit_places if who == owner]
        for place in range(each):
            if place not in taken:
                pooled[owner, :, place * LANE : (place + 1) * LANE] = jnp.zeros(
                    (regions, LANE), jnp.bfloat16
                )
    pool(0, 0, 2 * quarter)
    pooled_send(0, 0)
    pool(0, 2 * quarter, 3 * quarter)
    if shards > 1:
        lines[0][1](1)
    pool(0, 3 * quarter, groups)
    pooled_send(0, 1)
    for step in range(2, shards):
        lines[0][1](step)
        if step == shards - 2:
            lines[1][0]()
    if shards < 4:
        lines[1][0]()
    lines[0][2]()
    second_load[0].wait()
    first_layer(0)
    if shards > 1:
        lines[1][1](1)
    first_sums(0)
    head(0, info, between, all_params.at[1], all_bounds.at[1], spare_probs)
    second_load[1].start()
    start, relay, last, end = gather_of(0)
    start()

    pool(1, 0, quarter)
    if shards > 2:
        lines[1][1](2)
    relay()
    pool(1, quarter, 2 * quarter)
    pooled_send(1, 0)
    last()
    pool(1, 2 * quarter, 3 * quarter)
    for step in range(3, shards):
        lines[1][1](step)
    end()
    acts_end(0)
    pool(1, 3 * quarter, groups)
    pooled_send(1, 1)
    stores = (own_sums, rising, falling)
    weight_gradient, chain_start, chain_step, chain_end, chain_settle = shard_sums(
        me, shard, shards, gots.at[0], grads_all, acts_all, *stores, final.at[0], extra,
        rise_sem, fall_sem,
    )
    return_multiply, return_start, return_settle = pooled_return(
        me, shard, grads_all, weights.at[0], gots.at[0], first_back, back_sem.at[0], local_sem.at[9]
    )
    weight_gradient()
    chain_start()
    return_multiply()
    lines[1][2]()
    second_load[1].wait()
    first_layer(1)
    chain_step(0, True)
    chain_step(0, False)
    first_sums(1)
    return_start()
    for number in range(1, shards // 2):
        chain_step(number, True)
        chain_step(number, False)
    head(1, between, moved, spare_params, spare_bounds, probs)
    start, relay, last, end = gather_of(1)
    start()
    for number in range(shards // 2, shards):
        chain_step(number, True)
        chain_step(number, False)
    relay()
    chain_end()
    chain_settle()

    @pl.when(shard > 0)
    def _():
        pl.semaphore_signal(
            free_sem.at[0], inc=1,
            device_id=plane_place(me, lax.rem(shard + shards - 1, shards)),
            device_id_type=mesh_type,
        )

    @pl.when(shard < shards - 1)
    def _():
        pl.semaphore_signal(
            free_sem.at[1], inc=1, device_id=plane_place(me, lax.rem(shard + 1, shards)),
            device_id_type=mesh_type,
        )

    last()
    acts_end(1)
    end()

    slice_gather = plane_gather(
        chips, shard, final.at[0, pl.ds(0, depth)], slices, slice_sem, local_sem.at[10]
    )
    second_kept = pltpu.make_async_copy(
        final.at[1, pl.ds(0, depth)], second_final, local_sem.at[11]
    )
    head_gathers = [
        plane_gather(
            chips, shard, mixed.at[section], target, head_sem.at[section],
            local_sem.at[12 + section],
        )
        for section, target in enumerate((first_heads, second_heads))
    ]

    def mixed_copy(section, step):
        target = lax.rem(shard + step, shards)
        return pltpu.make_async_remote_copy(
            src_ref=final.at[section, pl.ds(depth, rows - depth)],
            dst_ref=mixed.at[section, :, pl.ds(pl.multiple_of(shard * width, LANE), width)],
            send_sem=mixed_sem.at[0, section, step], recv_sem=mixed_sem.at[1, section, step],
            device_id=plane_place(me, target), device_id_type=mesh_type,
        )

    def mix_start(section):
        for step in range(1, shards):
            mixed_copy(section, step).start()
        for at in range(shards):

            @pl.when(shard == at)
            def _():
                mixed[section, :, at * width : (at + 1) * width] = final[section, depth:, :]

    def mix_end(section):
        for step in range(1, shards):
            mixed_copy(section, step).wait()

    weight_gradient, chain_start, chain_step, chain_end, chain_settle = shard_sums(
        me, shard, shards, gots.at[1], grads_all, acts_all, *stores, final.at[1], extra,
        rise_sem, fall_sem,
    )
    back_multiply, back_start, back_settle = pooled_return(
        me, shard, grads_all, weights.at[1], pooled, second_back, back_sem.at[1], local_sem.at[14]
    )
    mix_start(0)
    slice_gather[0]()
    weight_gradient()

    @pl.when(shard < shards - 1)
    def _():
        pl.semaphore_wait(free_sem.at[0], 1)

    @pl.when(shard > 0)
    def _():
        pl.semaphore_wait(free_sem.at[1], 1)

    chain_start()
    back_multiply()
    mix_end(0)
    head_gathers[0][0]()
    chain_step(0, True)
    slice_gather[1]()
    head_gathers[0][1]()
    back_start()
    chain_step(0, False)
    for number in range(1, shards):
        chain_step(number, True)
        chain_step(number, False)
    slice_gather[2]()
    head_gathers[0][2]()
    chain_end()
    mix_start(1)
    second_kept.start()
    mix_end(1)
    head_gathers[1][0]()
    head_gathers[1][1]()
    head_gathers[1][2]()
    second_kept.wait()
    slice_gather[3]()
    head_gathers[0][3]()
    head_gathers[1][3]()
    return_settle()
    back_settle()
    chain_settle()


def run_cascade(
    owners, shards, info, maps, first_weight, first_bias, second_weight, second_bias, out_weight,
    out_bias,
):
    regions = info.shape[0]
    hidden = first_bias.shape[1]
    each, unused = unit_table(owners)
    depth = each * LANE
    rows, width, share = sum_sizes(owners, shards, depth, hidden)
    wide = 2 * hidden + LANE
    chips = owners // 2
    bf16 = jnp.bfloat16
    f32 = jnp.float32
    dma = pltpu.SemaphoreType.DMA
    vmem = pl.BlockSpec(memory_space=pltpu.VMEM)
    hbm = pl.BlockSpec(memory_space=pl.ANY)
    block = (owners, regions, depth)
    heads = (owners, rows - depth, hidden)
    shapes = [
        ((regions, LANE), f32),
        ((regions, LANE), f32),
        ((2, regions, LANE), f32),
        ((2, regions // GROUP, LANE), jnp.int32),
        (block, bf16),
        (block, bf16),
        ((owners, depth, width), bf16),
        ((depth, width), bf16),
        (heads, bf16),
        (heads, bf16),
    ]
    scratch = [
        pltpu.VMEM((2, shards, depth, width), bf16),
        pltpu.VMEM((hidden, hidden), bf16),
        pltpu.VMEM(block, bf16),
        pltpu.VMEM((2, *block), bf16),
        pltpu.VMEM((regions, LANE), f32),
        pltpu.VMEM((regions, LANE), f32),
        pltpu.VMEM((regions, LANE), f32),
        pltpu.VMEM((regions // GROUP, LANE), jnp.int32),
        pltpu.VMEM((chips, regions, hidden), f32),
        pltpu.VMEM((chips, regions, hidden), bf16),
        pltpu.VMEM((chips, regions, hidden), bf16),
        pltpu.VMEM((chips, regions, hidden), bf16),
        pltpu.VMEM((chips, regions, hidden), bf16),
        pltpu.VMEM((regions, hidden), f32),
        pltpu.VMEM((regions, hidden), f32),
        pltpu.VMEM((regions, LANE), f32),
        pltpu.VMEM((regions, wide), bf16),
        pltpu.VMEM((owners, regions, 2 * share), bf16),
        pltpu.VMEM((owners, regions, wide), bf16),
        pltpu.VMEM((owners, regions, 2 * share), bf16),
        pltpu.VMEM((shards, rows, width), bf16),
        pltpu.VMEM((shards, rows, width), bf16),
        pltpu.VMEM((shards, rows, width), bf16),
        pltpu.VMEM((2, rows, width), bf16),
        pltpu.VMEM((rows - depth - share, width), f32),
        pltpu.VMEM((2, rows - depth, hidden), bf16),
        pltpu.VMEM((POOL, GROUP, LANE), f32),
        pltpu.VMEM((POOL, GROUP, LANE), f32),
        pltpu.VMEM((POOL, GROUP, LANE), f32),
        pltpu.VMEM((BINS * GROUP, CH), f32),
        dma((2, 2, 2, shards)),
        dma((2, 2, 2, owners)),
        dma((2, 2, chips)),
        dma((2, 2, chips)),
        dma((2, 2, owners)),
        dma((2, 2, owners)),
        dma((2, 2, owners)),
        dma((2, shards)),
        dma((2, shards)),
        pltpu.SemaphoreType.REGULAR((2,)),
        dma((2, owners)),
        dma((2, 2, shards)),
        dma((2, 2, owners)),
        dma((15,)),
    ]
    return pl.pallas_call(
        functools.partial(cascade_kernel, owners, shards),
        out_shape=[jax.ShapeDtypeStruct(*shape) for shape in shapes],
        in_specs=[vmem, vmem, hbm, vmem, hbm, vmem, vmem, vmem],
        out_specs=[vmem] * 4 + [hbm] * 6,
        scratch_shapes=scratch,
        compiler_params=pltpu.CompilerParams(
            vmem_limit_bytes=62 << 20, collective_id=1, has_side_effects=True
        ),
        cost_estimate=SMALL,
        name="cascade",
    )(info, maps, first_weight, first_bias, second_weight, second_bias, out_weight, out_bias)


def box_frame(corners):
    box_width = corners[2] - corners[0]
    box_height = corners[3] - corners[1]
    return (corners[0] + 0.5 * box_width, corners[1] + 0.5 * box_height, box_width, box_height)


def unit_table(owners):
    each = -(-UNITS // owners)
    firsts = [min(owner * each, UNITS - each) for owner in range(owners)]
    return each, [(unit_no // each, unit_no - firsts[unit_no // each]) for unit_no in range(UNITS)]


def spread_regions(bounds, params, first, second):
    bounds = bounds.reshape(-1, LANE)
    params = params.reshape(-1, LANE)
    groups = bounds.shape[0] // 2
    owners = first.shape[0]
    each, places = unit_table(owners)
    width = BINS * GROUP
    block = (owners, GROUP, each * LANE)
    return pl.pallas_call(
        functools.partial(spread_kernel, places, 1.0 / 3.0, groups),
        grid_spec=pltpu.PrefetchScalarGridSpec(
            num_scalar_prefetch=1,
            grid=(2 * groups,),
            in_specs=[
                pl.BlockSpec((GROUP, LANE), lambda g, b: (g, 0)),
                pl.BlockSpec(block, lambda g, b: (0, jnp.minimum(g, groups - 1), 0)),
                pl.BlockSpec(block, lambda g, b: (0, jnp.maximum(g - groups, 0), 0)),
            ],
            out_specs=pl.BlockSpec((CELLS, CH), lambda g, b: (0, 0)),
            scratch_shapes=[
                pltpu.VMEM((SIDES[0], width), jnp.float32),
                pltpu.VMEM((width, CH), jnp.bfloat16),
            ],
        ),
        out_shape=jax.ShapeDtypeStruct((CELLS, CH), jnp.float32),
        compiler_params=pltpu.CompilerParams(vmem_limit_bytes=48 << 20),
        cost_estimate=SMALL,
        name="spread_regions",
    )(bounds, params, first, second)


def row_step(rows):
    blocks = rows // 16
    return 16 * max(number for number in range(1, 21) if blocks % number == 0)


def shard_sums(
    me, shard, shards, pooled, grads, acts, own, rising, falling, final, extra, rise_sem, fall_sem
):
    owners, regions, depth = pooled.shape
    both = owners * regions
    width = own.shape[2]
    rows = own.shape[1]
    hidden = width * shards
    share = acts.shape[2] // 2
    mesh_type = pl.DeviceIdType.MESH

    def weight_gradient():
        over_rows = (((0,), (0,)), ((), ()))

        def lay(first, size, block):
            for at in range(shards):
                own[at, pl.ds(first, size), :] = block[
                    :, at * width : (at + 1) * width
                ].astype(jnp.bfloat16)

        early = jnp.maximum(me * depth - (FEAT - depth), 0)

        def features(first, size):
            block = lax.dot_general(
                pooled[:, :, pl.ds(first, size)].reshape(both, size),
                grads[:, :, :hidden].reshape(both, hidden),
                over_rows, preferred_element_type=jnp.float32,
            )
            lay(pl.multiple_of(lax.rem(first + 2 * depth - early, depth), LANE), size, block)

        def step(number, carry):
            features(pl.multiple_of(number * CH, CH), CH)
            return carry

        lax.fori_loop(0, depth // CH, step, 0)
        if depth % CH:
            features(depth - depth % CH, depth % CH)
        block = lax.dot_general(
            acts[:, :, :share].reshape(both, share),
            grads[:, :, hidden : 2 * hidden].reshape(both, hidden),
            over_rows, preferred_element_type=jnp.float32,
        )
        lay(depth, share, block)
        block = lax.dot_general(
            acts[:, :, share:].reshape(both, share),
            grads[:, :, 2 * hidden :].reshape(both, LANE),
            over_rows, preferred_element_type=jnp.float32,
        )
        sums = jnp.dot(
            jnp.ones((8, both), jnp.bfloat16), grads[...].reshape(both, 2 * hidden + LANE),
            preferred_element_type=jnp.float32,
        )
        part = share // shards
        for at in range(shards):
            extra[...] = jnp.zeros_like(extra)
            extra[:part, :LANE] = block[at * part : (at + 1) * part]
            for number in range((2 * hidden + LANE) // LANE):
                row, lane = (part + number, 0) if width == LANE else (number, LANE)
                extra[row : row + 1, lane : lane + LANE] = sums[
                    :1, number * LANE : (number + 1) * LANE
                ]
            own[at, depth + share :, :] = extra[...].astype(jnp.bfloat16)

    step_rows = row_step(rows)

    def by_rows(work):
        def step(number, carry):
            work(pl.ds(pl.multiple_of(number * step_rows, 16), step_rows))
            return carry

        lax.fori_loop(0, rows // step_rows, step, 0)

    def rise_copy(at):
        return pltpu.make_async_remote_copy(
            src_ref=rising.at[at], dst_ref=rising.at[at],
            send_sem=rise_sem.at[0, at], recv_sem=rise_sem.at[1, at],
            device_id=plane_place(me, lax.rem(shard + 1, shards)), device_id_type=mesh_type,
        )

    def fall_copy(at):
        return pltpu.make_async_remote_copy(
            src_ref=falling.at[at], dst_ref=falling.at[at],
            send_sem=fall_sem.at[0, at], recv_sem=fall_sem.at[1, at],
            device_id=plane_place(me, lax.rem(shard + shards - 1, shards)),
            device_id_type=mesh_type,
        )

    def add_own(at, stream):
        def work(place):
            stream[at, place, :] = (
                stream[at, place, :].astype(jnp.float32)
                + own[at, place, :].astype(jnp.float32)
            ).astype(jnp.bfloat16)

        by_rows(work)

    def rise_first(at):
        return pltpu.make_async_remote_copy(
            src_ref=own.at[at], dst_ref=rising.at[at],
            send_sem=rise_sem.at[0, at], recv_sem=rise_sem.at[1, at],
            device_id=plane_place(me, lax.rem(shard + 1, shards)), device_id_type=mesh_type,
        )

    def fall_first(at):
        return pltpu.make_async_remote_copy(
            src_ref=own.at[at], dst_ref=falling.at[at],
            send_sem=fall_sem.at[0, at], recv_sem=fall_sem.at[1, at],
            device_id=plane_place(me, lax.rem(shard + shards - 1, shards)),
            device_id_type=mesh_type,
        )

    def chain_start():
        for number in range(shards - 1):
            at = shards - 1 - number

            @pl.when(shard == 0)
            def _():
                rise_first(at).start()

            @pl.when(shard == shards - 1)
            def _():
                fall_first(number).start()

    def pass_on(at, stream, copy, ahead):
        @pl.when(ahead)
        def _():
            copy(at).wait_recv()
            add_own(at, stream)
            copy(at).start()

    def chain_step(number, near):
        up = shards - 1 - number
        down = number
        low = shard < shards // 2
        rises = low if near else jnp.logical_not(low)
        falls = jnp.logical_not(rises)
        inner = jnp.logical_and(shard > 0, shard < shards - 1)
        rises = jnp.logical_and(rises, jnp.logical_and(inner, shard < up))
        falls = jnp.logical_and(falls, jnp.logical_and(inner, shard > down))
        pass_on(up, rising, rise_copy, rises)
        pass_on(down, falling, fall_copy, falls)

    def chain_end():
        def work(place):
            final[place, :] = own[shard, place, :]

        def work_up(place):
            total = own[shard, place, :].astype(jnp.float32)
            total = total + rising[shard, place, :].astype(jnp.float32)
            final[place, :] = total.astype(jnp.bfloat16)

        def work_down(place):
            total = own[shard, place, :].astype(jnp.float32)
            total = total + falling[shard, place, :].astype(jnp.float32)
            final[place, :] = total.astype(jnp.bfloat16)

        def work_both(place):
            total = own[shard, place, :].astype(jnp.float32)
            total = total + rising[shard, place, :].astype(jnp.float32)
            total = total + falling[shard, place, :].astype(jnp.float32)
            final[place, :] = total.astype(jnp.bfloat16)

        if shards == 1:
            by_rows(work)
            return

        @pl.when(shard > 0)
        def _():
            rise_copy(shard).wait_recv()

        @pl.when(shard < shards - 1)
        def _():
            fall_copy(shard).wait_recv()

        @pl.when(shard == 0)
        def _():
            by_rows(work_down)

        @pl.when(shard == shards - 1)
        def _():
            by_rows(work_up)

        @pl.when(jnp.logical_and(shard > 0, shard < shards - 1))
        def _():
            by_rows(work_both)

    def chain_settle():
        for at in range(shards):

            @pl.when(jnp.logical_and(shard < at, shard == 0))
            def _():
                rise_first(at).wait_send()

            @pl.when(jnp.logical_and(shard < at, shard > 0))
            def _():
                rise_copy(at).wait_send()

            @pl.when(jnp.logical_and(shard > at, shard == shards - 1))
            def _():
                fall_first(at).wait_send()

            @pl.when(jnp.logical_and(shard > at, shard < shards - 1))
            def _():
                fall_copy(at).wait_send()

    return weight_gradient, chain_start, chain_step, chain_end, chain_settle


def pooled_return(me, shard, grads, weight, sent, back, back_sem, own_sem):
    owners, regions, depth = sent.shape
    shards, unused, width = weight.shape
    both = owners * regions

    def back_copy(step):
        target = lax.rem(me + step, owners)
        return pltpu.make_async_remote_copy(
            src_ref=sent.at[target], dst_ref=back.at[me],
            send_sem=back_sem.at[0, step], recv_sem=back_sem.at[1, step],
            device_id=plane_place(target, shard), device_id_type=pl.DeviceIdType.MESH,
        )

    own = pltpu.make_async_copy(sent.at[me], back.at[me], own_sem)

    def multiply():
        def columns(first, size):
            at = pl.ds(first, size)
            block = sum(
                lax.dot_general(
                    grads[:, :, part * width : (part + 1) * width].reshape(both, width),
                    weight[part, at, :],
                    (((1,), (1,)), ((), ())),
                    preferred_element_type=jnp.float32,
                )
                for part in range(shards)
            )
            sent[:, :, at] = block.astype(jnp.bfloat16).reshape(owners, regions, size)

        def step(number, carry):
            columns(pl.multiple_of(number * CH, CH), CH)
            return carry

        lax.fori_loop(0, depth // CH, step, 0)
        if depth % CH:
            columns(depth - depth % CH, depth % CH)

    def start():
        for step in range(1, owners):
            back_copy(step).start()
        own.start()

    def settle():
        own.wait()

        def work(step, carry):
            back_copy(step).wait()
            return carry

        lax.fori_loop(1, owners, work, 0)

    return multiply, start, settle


def sum_sizes(owners, shards, depth, hidden):
    width = hidden // shards
    share = hidden // owners
    part = share // shards
    extra = max(part, 32) if width > LANE else part + 32
    return depth + share + -(-extra // 16) * 16, width, share


def widen_kernel(every, *refs):
    refs[-1][0] = every[...].astype(jnp.float32)


def widen_slices(every, section_no, whole=None):
    owners, depth, width = every.shape
    rows = FEAT // 7
    given = () if whole is None else (whole,)
    return pl.pallas_call(
        widen_kernel,
        grid=(7,),
        in_specs=[pl.BlockSpec((rows, width), lambda at: (at, 0))]
        + [pl.BlockSpec(memory_space=pl.ANY)] * len(given),
        out_specs=pl.BlockSpec((1, rows, width), lambda at: (section_no, at, 0)),
        out_shape=jax.ShapeDtypeStruct((2, FEAT, width), jnp.float32),
        input_output_aliases={1: 0} if given else {},
        cost_estimate=SMALL,
        name="widen_slices",
    )(every.reshape(owners * depth, width), *given)


def widen_heads_kernel(share, shards, first, second, second_grad, out_grad, sums):
    owners = first.shape[0]
    part = share // shards
    width = first.shape[2] // shards
    for section, heads in enumerate((first, second)):
        for owner in range(owners):
            rows = slice(owner * share, (owner + 1) * share)
            second_grad[section, rows, :] = heads[owner, :share].astype(jnp.float32)
            for at in range(shards):
                rows = slice(owner * share + at * part, owner * share + (at + 1) * part)
                out_grad[section, rows, :] = heads[
                    owner, share : share + part, at * width : at * width + LANE
                ].astype(jnp.float32)
        row, lane = (share, LANE) if width > LANE else (share + part, 0)
        sums[section] = heads[0, row : row + sums.shape[1], lane : lane + LANE].astype(jnp.float32)


def widen_heads(share, shards, first, second):
    hidden = first.shape[2]
    count = -(-(2 * hidden + LANE) // (LANE * 8)) * 8
    return pl.pallas_call(
        functools.partial(widen_heads_kernel, share, shards),
        out_shape=[
            jax.ShapeDtypeStruct((2, hidden, hidden), jnp.float32),
            jax.ShapeDtypeStruct((2, hidden, LANE), jnp.float32),
            jax.ShapeDtypeStruct((2, count, LANE), jnp.float32),
        ],
        compiler_params=pltpu.CompilerParams(vmem_limit_bytes=48 << 20),
        cost_estimate=SMALL,
        name="widen_heads",
    )(first, second)


def per_device(
    pyramid,
    proposals,
    levels,
    labels,
    targets,
    buckets,
    first_weight,
    first_bias,
    second_weight,
    second_bias,
    class_weight,
    class_bias,
    box_weight,
    box_bias,
):
    owners = lax.axis_size("plane") * 2
    shards = lax.axis_size("mp")
    regions = levels.shape[1]
    hidden = first_bias.shape[1]
    share = hidden // owners

    index = jnp.arange(regions, dtype=jnp.int32)
    live = (index < regions // 2 + buckets[0] * (regions // 8)).astype(jnp.int32)
    order = (levels[0] * 1024 + proposals[0, 1] + proposals[0, 3]) * regions + index
    rank = jnp.sum((order[:, None] > order[None, :]).astype(jnp.int32), axis=1)
    moved = rank[None, :] == index[:, None]
    live_count = jnp.broadcast_to(jnp.sum(live), live.shape)
    moving = live * (labels[0] > 0).astype(jnp.int32)
    columns = jnp.concatenate(
        [proposals[0], targets[0], levels, labels, live[None], live_count[None], moving[None]],
        axis=0,
    ).astype(jnp.float32)
    info = jnp.sum(jnp.where(moved[:, None, :], columns[None], 0.0), axis=2)
    info = jnp.pad(info, ((0, 0), (0, LANE - columns.shape[0])))

    out_width = ((0, 0), (0, 0), (0, LANE - CLS - 4))
    out_weight = jnp.pad(jnp.concatenate([class_weight, box_weight], axis=2), out_width)
    out_bias = jnp.pad(jnp.concatenate([class_bias, box_bias], axis=1), out_width[1:])

    decoded_info, probs, params, bounds, *rest = run_cascade(
        owners, shards, info, pyramid[0], first_weight, first_bias, second_weight, second_bias,
        out_weight, out_bias,
    )
    first_back, second_back, first_all, second_final, *heads = rest
    pyramid_part = spread_regions(bounds, params, first_back, second_back)
    second_all = lax.all_gather(second_final, ("plane", "core"), axis=0)
    weight_total = widen_slices(first_all, 0)
    weight_total = widen_slices(second_all, 1, weight_total)
    second_grad, out_grad, sums = widen_heads(share, shards, *heads)
    sums = sums.reshape(2, -1)
    result = jnp.concatenate([probs[:, :CLS], decoded_info[:, :4]], axis=1)
    result = jnp.einsum(
        "pr,pc->rc", moved.astype(jnp.float32), result, precision=lax.Precision.HIGHEST
    )
    return (
        result[None, :, :CLS],
        result[:, CLS:].T[None],
        pyramid_part[None],
        weight_total,
        sums[:, :hidden],
        second_grad,
        sums[:, hidden : 2 * hidden],
        out_grad[:, :, :CLS],
        sums[:, 2 * hidden : 2 * hidden + CLS],
        out_grad[:, :, CLS : CLS + 4],
        sums[:, 2 * hidden + CLS : 2 * hidden + CLS + 4],
    )


def solution(mesh):
    chips = mesh.shape["dp"] // 2
    layout = Mesh(
        mesh.devices.reshape(chips, 2, mesh.shape["mp"]), ("plane", "core", "mp")
    )
    images = ("plane", "core", "mp")
    rows = P(images, None, None)
    columns = P(None, None, "mp")
    return jax.shard_map(
        per_device,
        mesh=layout,
        in_specs=(rows, rows, P(images, None), P(images, None), rows, P(images), columns)
        + (P(),) * 7,
        out_specs=(rows, rows, rows, columns) + (P(),) * 7,
        check_vma=False,
    )
```
